1024 devices in a mesh: pipe: 16 (over x, core), expert: 16 (over y_hi, z), dp: 4 (over y_lo).
Axes of the slice: x: 8, y: 8 (y_hi: 2, y_lo: 4; y = y_hi * 4 + y_lo), z: 8, core: 2. Of those that a mesh axis runs over, the one named last changes fastest.
Arguments:
- cotangent: bfloat16 [16, 8192, 3584], P('pipe', ('expert', 'dp')), may hold values from -6 to 6
- combine: float32 [16, 8192, 1], P('pipe', ('expert', 'dp')), may hold values from 0.1 to 1
- routes: int32 [16, 8192, 1], P('pipe', ('expert', 'dp')), may hold values from 0 to 15; in each aligned block of 128 rows (0 to 127, 128 to 255, ..., all dimensions but the last counted through in order) at most 12 rows name the same one
- saved_hidden: bfloat16 [16, 16, 4, 192, 1024], P('pipe', 'expert', 'dp'), may hold values from -0.359375 to 0.359375
Outputs:
- grad_down: bfloat16 [16, 16, 512, 3584], P('pipe', 'expert', None, 'dp')
The draws below stay inside these ranges and needn't reach their ends.
Inputs may be any that keep to these rules, and one draw needn't show every extreme that they name: `routes`: among the rows of one device no expert is named more than 12 times, and in every draw some device names some expert exactly 12 times.
All inputs are finite; a program needn't handle non-finite values.
Results may differ from the reference program's by a relative error of at most 0.0059.
Values may be sent and summed in bfloat16 or wider, within the bound.
A program may use at most 64 MiB of HBM per device.

```python
import math
import jax
import jax.numpy as jnp
import numpy as np
from jax import lax

D = 3584
FF = 1024
TOK = 128
ROUTES = 1
EXPERTS = 16
CAP = 12
SLOTS = 192
TOKENS = 8192
N_PIPE = 16
N_EXPERT = 16
N_DP = 4


def block_scale(key, shape, split, least, high):
    factor_of = 1.0
    for dim, parts in split:
        steps = jax.random.uniform(jax.random.fold_in(jax.random.fold_in(key, 6), dim), (parts,), jnp.float32, least / len(split), high / len(split))
        factor_of = factor_of * jnp.repeat(jnp.exp(steps), shape[dim] // parts).reshape((-1,) + (1,) * (len(shape) - 1 - dim))
    return factor_of


def shared_out(key, own, number, rows, number_of, top, limit, slope):
    ranking = jax.random.permutation(key, number_of)
    packed, common = shares(number_of, rows * top, limit, slope, True), shares(number_of, rows * top, limit, slope, False)
    places = jnp.arange(number_of)

    def named(sizes, offset_by):
        used = int((sizes > 0).sum())
        fixed = max(1, used // 4)
        moved = fixed + (places - fixed + offset_by * (used - fixed)) % max(1, number_of - fixed)
        return jnp.zeros((number_of,), jnp.int32).at[ranking[jnp.where(places < fixed, places, moved)]].set(jnp.asarray(sizes, jnp.int32))

    sizes = jnp.where(number % 4 == 0, named(packed, number // 4), named(common, number - number // 4 - 1))
    mixed = jax.random.permutation(jax.random.fold_in(own, 3), number_of)
    source_of, sink = mixed[0:number_of // 2 * 2:2], mixed[1:number_of // 2 * 2:2]
    room = jnp.minimum(sizes[source_of] - 1, limit - sizes[sink]) // 2
    room = jnp.where((source_of == ranking[0]) | (sink == ranking[0]) | (sizes[sink] == 0), 0, jnp.maximum(room, 0))
    moved = jax.random.randint(jax.random.fold_in(own, 4), (number_of // 2,), 0, 1 << 20) % (room + 1)
    sizes = sizes.at[source_of].add(-moved).at[sink].add(moved)
    items = jnp.searchsorted(jnp.cumsum(sizes), jnp.arange(rows * top), side="right").astype(jnp.int32)
    grid = items.reshape(top, rows).T
    grid = grid[jax.random.permutation(jax.random.fold_in(own, 1), rows)]
    offset_by = jax.random.randint(jax.random.fold_in(own, 2), (rows, 1), 0, top)
    return jnp.take_along_axis(grid, (jnp.arange(top)[None, :] + offset_by) % top, axis=1)


def shares(number_of, total, limit, lean, full):
    loads = [(1 << 20) // math.isqrt(grade ** lean) + 1 for grade in range(1, number_of + 1)]
    largest = limit if full else min(limit, max(-(-total // number_of), total * loads[0] // sum(loads)))
    least = 1 if total - largest >= number_of - 1 else 0
    counts, spare = [largest] + [least] * (number_of - 1), total - largest - least * (number_of - 1)
    while spare > 0:
        free = [i for i in range(1, number_of) if counts[i] < largest] or [i for i in range(1, number_of) if counts[i] < limit]
        pool, remaining = sum([loads[i] for i in free]), spare
        for i in free:
            extra = min(limit - counts[i], max(1, remaining * loads[i] // pool), spare)
            counts[i] = counts[i] + extra
            spare = spare - extra
    return np.array(counts)


def bell_draw(key, shape, spread, reach, pieces=(), held_as=jnp.bfloat16):
    entries = spread * jax.random.normal(key, shape, jnp.float32)
    if pieces:
        entries = entries * block_scale(key, shape, pieces, -0.22, 0.18)
    return jnp.clip(entries, -reach, reach).astype(held_as)


def setup_inputs(seed: int = 0) -> dict:
    streams_of = jax.random.split(jax.random.key(seed), 5)
    cotangent = bell_draw(streams_of[0], (N_PIPE, TOKENS, D), 1.0, 6.0, ((0, 16), (1, 64)))
    combine = jnp.clip(jnp.exp(math.log(1.0) - 2.3025851 * jax.random.uniform(streams_of[1], (N_PIPE, TOKENS, ROUTES), jnp.float32) ** block_scale(streams_of[1], (N_PIPE, TOKENS, ROUTES), ((0, 16), (1, 64)), -0.2, 0.2)), 0.1, 1.0)
    routes_keys = jax.random.split(jax.random.fold_in(streams_of[2], 1), N_PIPE * TOKENS // TOK)
    routes_turns = jax.random.permutation(jax.random.fold_in(streams_of[2], 3), N_PIPE * TOKENS // TOK)
    routes = jax.vmap(lambda own, number: shared_out(jax.random.fold_in(streams_of[2], 2), own, number, TOK, EXPERTS, ROUTES, CAP, 2))(routes_keys, routes_turns).reshape((N_PIPE, TOKENS, ROUTES))
    saved_hidden = bell_draw(streams_of[3], (N_PIPE, EXPERTS, N_DP, SLOTS, FF), 0.06, 0.359375, ((0, 16), (1, 16), (2, 4)))
    return dict(cotangent=cotangent, combine=combine, routes=routes, saved_hidden=saved_hidden)


def slot_table(chosen, expert_count, capacity):
    labels = jnp.arange(expert_count, dtype=jnp.int32)
    matches = (chosen[:, None] == labels[None, :]).astype(jnp.int32)
    earlier = jnp.cumsum(matches, axis=0) - matches
    position = lax.optimization_barrier(jnp.sum(earlier * matches, axis=1)).astype(jnp.int32)
    target = (chosen * capacity + position).astype(jnp.int32)
    columns = jnp.arange(expert_count * capacity, dtype=jnp.int32)
    return (target[:, None] == columns[None, :]).astype(jnp.bfloat16)

def route_rows(upstream, mixing, chosen, expert_count, capacity):
    feature_count = upstream.shape[1]
    values = (mixing[:, :, None] * upstream.astype(jnp.float32)[:, None, :]).reshape(-1, feature_count).astype(jnp.bfloat16)
    slot_matrix = slot_table(chosen.reshape(-1), expert_count, capacity)
    placed = lax.dot_general(slot_matrix, values, (((0,), (0,)), ((), ())), preferred_element_type=jnp.float32)
    return placed.astype(jnp.bfloat16)

def reference(cotangent, combine, routes, saved_hidden):
    upstream = cotangent.reshape(N_PIPE, N_EXPERT, N_DP, TOK, D)
    mixing = combine.reshape(N_PIPE, N_EXPERT, N_DP, TOK, ROUTES)
    chosen = routes.reshape(N_PIPE, N_EXPERT, N_DP, TOK, ROUTES)

    def one_device(rows_in, weights_in, routes_in):
        return route_rows(rows_in, weights_in, routes_in, N_EXPERT, CAP)
    sender = jax.vmap(jax.vmap(one_device))

    def section_rows(section):
        return sender(upstream[section], mixing[section], chosen[section])

    def replica_grad(outgoing, hidden_section, expert):
        column_block = lax.dynamic_slice_in_dim(outgoing, (expert * CAP).astype(jnp.int32), CAP, 2)
        column_block = jnp.transpose(column_block, (1, 0, 2, 3)).reshape(N_DP * N_EXPERT * CAP, D)
        hidden_rows = hidden_section[expert].reshape(N_DP * N_EXPERT * CAP, FF)
        product = lax.dot_general(hidden_rows, column_block, (((0,), (0,)), ((), ())), preferred_element_type=jnp.float32)
        return product.astype(jnp.bfloat16)

    def pair_sum(lower_section):
        upper_section = (N_PIPE - 1 - lower_section).astype(jnp.int32)
        first = section_rows(lower_section)
        second = section_rows(upper_section)
        first_hidden = saved_hidden[lower_section]
        second_hidden = saved_hidden[upper_section]

        def per_expert(expert):
            total = replica_grad(first, first_hidden, expert).astype(jnp.float32) + replica_grad(second, second_hidden, expert).astype(jnp.float32)
            return (total[:FF // 2].astype(jnp.bfloat16), total[FF // 2:].astype(jnp.bfloat16))
        return lax.map(per_expert, jnp.arange(N_EXPERT, dtype=jnp.int32))
    lower_half, upper_half = lax.map(pair_sum, jnp.arange(N_PIPE // 2, dtype=jnp.int32))
    return jnp.concatenate([lower_half, upper_half[::-1]], axis=0)
```

```python
import functools

import jax
import jax.numpy as jnp
import numpy as np
from jax import lax
from jax.experimental import pallas as pl
from jax.experimental.pallas import tpu as pltpu
from jax.sharding import PartitionSpec as P

MESH = pl.DeviceIdType.MESH
CHUNKS = (256, 256, 256, 128)
RING = (1, 7, 2, 6, 3, 5, 4)
Z = 8


def regroup_matrix(replicas, highs, capacity):
    rows = replicas * highs * Z * capacity
    order = np.arange(rows).reshape(replicas, highs, Z, capacity).transpose(2, 0, 1, 3).reshape(-1)
    matrix = np.zeros((rows, rows), np.float32)
    matrix[np.arange(rows), order] = 1
    return matrix


def kernel(
    sections, experts, replicas,
    cot_hbm, combine_hbm, routes_hbm, hidden_hbm, perm_hbm, out_hbm,
    cot, combine, routes, perm, slot, hm, ho, htm, hto, *rest,
):
    n = len(CHUNKS)
    ysend, yrecv, zsend, zrecv, xsend, xrecv, own, outb = (rest[i * n:(i + 1) * n] for i in range(8))
    load_sem, self_sem, ys, yr, zs, zr, xs, xr, hs, hr, out_sem = rest[8 * n:]
    highs = experts // Z
    ring = highs * replicas
    tokens, features = cot.shape
    half = hm.shape[2]
    share = features // replicas
    offsets = [sum(CHUNKS[:c]) for c in range(n)]

    p, e, d = lax.axis_index("pipe"), lax.axis_index("expert"), lax.axis_index("dp")
    high, z = e // Z, e % Z
    y = high * replicas + d
    mine = d * highs + high
    keep = jnp.where(p < sections // 2, 0, 1)

    def y_peer(step):
        other = (y + step) % ring
        oh, od = other // replicas, other % replicas
        return (p, oh * Z + z, od), od * highs + oh

    def z_peer(step):
        other = (z + step) % Z
        return (p, high * Z + other, d), other

    mirror = (sections - 1 - p, e, d)

    barrier = pltpu.get_barrier_semaphore()
    peers = [y_peer(s)[0] for s in RING] + [z_peer(s)[0] for s in RING] + [mirror]
    for peer in peers:
        pl.semaphore_signal(barrier, inc=1, device_id=peer, device_id_type=MESH)

    cols_m = pl.ds(pl.multiple_of((1 - keep) * half, half), half)
    cols_o = pl.ds(pl.multiple_of(keep * half, half), half)
    loads = [
        pltpu.make_async_copy(routes_hbm, routes, load_sem.at[0]),
        pltpu.make_async_copy(combine_hbm, combine, load_sem.at[1]),
        pltpu.make_async_copy(cot_hbm, cot, load_sem.at[2]),
        pltpu.make_async_copy(perm_hbm, perm, load_sem.at[3]),
        pltpu.make_async_copy(hidden_hbm.at[:, cols_m], hm.at[d], load_sem.at[4]),
        pltpu.make_async_copy(hidden_hbm.at[:, cols_o], ho.at[d], load_sem.at[5]),
    ]
    for load in loads:
        load.start()

    loads[0].wait()
    chosen = routes[...]
    match = (lax.broadcasted_iota(jnp.int32, (experts, tokens), 0) == chosen).astype(jnp.float32)
    before = (
        lax.broadcasted_iota(jnp.int32, (tokens, tokens), 0)
        < lax.broadcasted_iota(jnp.int32, (tokens, tokens), 1)
    ).astype(jnp.bfloat16)
    earlier = jnp.dot(match.astype(jnp.bfloat16), before, preferred_element_type=jnp.float32)
    position = jnp.sum(earlier * match, axis=0, keepdims=True)
    slots = slot.shape[0]
    capacity = slots // experts
    target = chosen.astype(jnp.float32) * capacity + position
    slot[...] = (
        lax.broadcasted_iota(jnp.int32, (slots, tokens), 0).astype(jnp.float32) == target
    ).astype(jnp.bfloat16)
    loads[1].wait()
    eye = lax.broadcasted_iota(jnp.int32, (tokens, tokens), 0) == lax.broadcasted_iota(
        jnp.int32, (tokens, tokens), 1
    )
    weight = jnp.sum(jnp.where(eye, combine[...], 0.0), axis=1, keepdims=True)
    loads[2].wait()

    def place(c):
        w = CHUNKS[c]
        for q in range(replicas):
            at = q * share + offsets[c]
            block = (weight * cot[:, at:at + w].astype(jnp.float32)).astype(jnp.bfloat16)
            placed = jnp.dot(slot[...], block, preferred_element_type=jnp.float32).astype(jnp.bfloat16)
            for h in range(highs):
                rows = slots // highs
                ysend[c][q * highs + h] = placed[h * rows:(h + 1) * rows]

    def y_copy(c, step, arriving=False):
        peer, theirs = y_peer(step)
        slot_of = theirs if arriving else mine
        return pltpu.make_async_remote_copy(
            src_ref=ysend[c].at[theirs], dst_ref=yrecv[c].at[slot_of],
            send_sem=ys.at[c, theirs], recv_sem=yr.at[c, slot_of], device_id=peer, device_id_type=MESH)

    def y_self(c):
        return pltpu.make_async_copy(ysend[c].at[mine], yrecv[c].at[mine], self_sem.at[0, c])

    def y_start(c):
        for s in RING:
            y_copy(c, s).start()
        y_self(c).start()

    def z_copy(c, step, arriving=False):
        peer, theirs = z_peer(step)
        slot_of = theirs if arriving else z
        return pltpu.make_async_remote_copy(
            src_ref=zsend[c].at[theirs], dst_ref=zrecv[c].at[slot_of],
            send_sem=zs.at[c, theirs], recv_sem=zr.at[c, slot_of], device_id=peer, device_id_type=MESH)

    def z_self(c):
        return pltpu.make_async_copy(zsend[c].at[z], zrecv[c].at[z], self_sem.at[1, c])

    def regroup(c):
        for s in RING:
            y_copy(c, s, True).wait_recv()
        y_self(c).wait()
        rows = yrecv[c].shape[0] * yrecv[c].shape[1]
        arrived = yrecv[c][...].reshape(rows, CHUNKS[c])
        moved = jnp.dot(perm[...], arrived, preferred_element_type=jnp.float32)
        zsend[c][...] = moved.astype(jnp.bfloat16).reshape(zsend[c].shape)
        for s in RING:
            z_copy(c, s).start()
        z_self(c).start()

    def x_copy(c):
        return pltpu.make_async_remote_copy(
            src_ref=xsend[c], dst_ref=xrecv[c], send_sem=xs.at[c], recv_sem=xr.at[c],
            device_id=mirror, device_id_type=MESH)

    def rows_of(c):
        return zrecv[c][...].reshape(zrecv[c].shape[0] * zrecv[c].shape[1], CHUNKS[c])

    def give(c):
        for s in RING:
            z_copy(c, s, True).wait_recv()
        z_self(c).wait()
        xsend[c][...] = jnp.dot(
            htm[...], rows_of(c), preferred_element_type=jnp.float32).astype(jnp.bfloat16)
        x_copy(c).start()

    held = (hm, ho)
    cols = (cols_m, cols_o)

    def h_copy(part, origin, way, own_block):
        return pltpu.make_async_remote_copy(
            src_ref=hidden_hbm.at[:, cols[part]] if own_block else held[part].at[origin],
            dst_ref=held[part].at[origin],
            send_sem=hs.at[part, origin, way], recv_sem=hr.at[part, origin],
            device_id=(p, e, d + 1 if way else d - 1), device_id_type=MESH)

    def h_round(part, k):
        if k:
            @pl.when(d >= k)
            def _():
                h_copy(part, d - k, 1, False).wait_recv()

        @pl.when((d >= k) & (d < replicas - 1))
        def _():
            h_copy(part, d - k, 1, k == 0).start()

        if k:
            @pl.when(d + k < replicas)
            def _():
                h_copy(part, d + k, 0, False).wait_recv()

        @pl.when((d + k < replicas) & (d > 0))
        def _():
            h_copy(part, d + k, 0, k == 0).start()

    def h_sent(part, k):
        @pl.when((d >= k) & (d < replicas - 1))
        def _():
            h_copy(part, d - k, 1, k == 0).wait_send()

        @pl.when((d + k < replicas) & (d > 0))
        def _():
            h_copy(part, d + k, 0, k == 0).wait_send()

    def turn(part, to):
        rows = held[part].shape[0] * held[part].shape[1]
        to[...] = lax.dot_general(
            held[part][...].reshape(rows, half), perm[...], (((0,), (0,)), ((), ())),
            preferred_element_type=jnp.float32).astype(jnp.bfloat16)

    place(0)
    pl.semaphore_wait(barrier, len(peers))
    h_round(0, 0)
    y_start(0)
    for c in range(1, n):
        place(c)
    y_start(1)
    h_round(0, 1)
    h_round(0, 2)
    loads[3].wait()
    regroup(0)
    y_start(2)
    h_round(0, 3)
    loads[4].wait()
    turn(0, htm)
    regroup(1)
    y_start(3)
    h_round(1, 0)
    give(0)
    regroup(2)
    h_round(1, 1)
    give(1)
    regroup(3)
    h_round(1, 2)
    give(2)
    give(3)
    h_round(1, 3)
    loads[5].wait()
    turn(1, hto)
    for c in range(n):
        own[c][...] = jnp.dot(
            hto[...], rows_of(c), preferred_element_type=jnp.float32).astype(jnp.bfloat16)

    def result(c):
        return pltpu.make_async_copy(
            outb[c], out_hbm.at[:, pl.ds(offsets[c], CHUNKS[c])], out_sem.at[c])

    for c in range(n):
        x_copy(c).wait_recv()
        outb[c][...] = (
            own[c][...].astype(jnp.float32) + xrecv[c][...].astype(jnp.float32)
        ).astype(jnp.bfloat16)
        result(c).start()
    for c in range(n):
        for s in RING:
            y_copy(c, s).wait_send()
            z_copy(c, s).wait_send()
        x_copy(c).wait_send()
    for part in range(2):
        for k in range(replicas - 1):
            h_sent(part, k)
    for c in range(n):
        result(c).wait()


def solution(mesh):
    sections, experts, replicas = (mesh.shape[a] for a in ("pipe", "expert", "dp"))

    def on_device(cotangent, combine, routes, saved_hidden):
        tokens, features = cotangent.shape[1:]
        slots, hidden_units = saved_hidden.shape[3:]
        half, share = hidden_units // 2, features // replicas
        highs = experts // Z
        rows = slots * replicas
        capacity = slots // experts
        matrix = regroup_matrix(replicas, highs, capacity)
        perm = jnp.asarray(matrix, jnp.bfloat16)
        n = len(CHUNKS)
        bf16 = jnp.bfloat16
        dma = pltpu.SemaphoreType.DMA
        each = lambda lead: [pltpu.VMEM(lead + (w,), bf16) for w in CHUNKS]
        block = (replicas * highs, rows // (replicas * highs))
        zblock = (Z, rows // Z)
        out = pl.pallas_call(
            functools.partial(kernel, sections, experts, replicas),
            out_shape=jax.ShapeDtypeStruct((half, share), bf16),
            in_specs=[pl.BlockSpec(memory_space=pl.ANY)] * 5,
            out_specs=pl.BlockSpec(memory_space=pl.ANY),
            scratch_shapes=[
                pltpu.VMEM((tokens, features), bf16),
                pltpu.VMEM((1, tokens), jnp.float32),
                pltpu.VMEM((1, tokens), jnp.int32),
                pltpu.VMEM((rows, rows), bf16),
                pltpu.VMEM((slots, tokens), bf16),
                pltpu.VMEM((replicas, slots, half), bf16),
                pltpu.VMEM((replicas, slots, half), bf16),
                pltpu.VMEM((half, rows), bf16),
                pltpu.VMEM((half, rows), bf16),
                *each(block), *each(block), *each(zblock), *each(zblock),
                *each((half,)), *each((half,)), *each((half,)), *each((half,)),
                dma((6,)), dma((2, n)),
                dma((n, replicas * highs)), dma((n, replicas * highs)),
                dma((n, Z)), dma((n, Z)),
                dma((n,)), dma((n,)),
                dma((2, replicas, 2)), dma((2, replicas)),
                dma((n,)),
            ],
            compiler_params=pltpu.CompilerParams(
                collective_id=0, has_side_effects=True, vmem_limit_bytes=60 << 20),
        )(
            cotangent[0], combine.reshape(1, tokens), routes.reshape(1, tokens),
            saved_hidden[0, 0, 0], perm,
        )
        return out[None, None]

    return jax.shard_map(
        on_device,
        mesh=mesh,
        in_specs=(
            P("pipe", ("expert", "dp"), None),
            P("pipe", ("expert", "dp"), None),
            P("pipe", ("expert", "dp"), None),
            P("pipe", "expert", "dp", None, None),
        ),
        out_specs=P("pipe", "expert", None, "dp"),
        check_vma=False,
    )
```

```python
import functools

import jax
import jax.numpy as jnp
import numpy as np
from jax import lax
from jax.experimental import pallas as pl
from jax.experimental.pallas import tpu as pltpu
from jax.sharding import PartitionSpec as P

MESH = pl.DeviceIdType.MESH
CHUNKS = (128,) * 7
PARTS = 4
RING = (1, 7, 2, 6, 3, 5, 4)
Z = 8
PLAN = (
    "h00", "h10", "y0", "y1", "h01", "h11", "y2", "h02", "h12", "z0", "y3", "z1", "h03", "t0", "h13", "t1",
    "x00", "x01", "y4", "z2", "x10", "x11", "y5", "z3", "x20", "x21", "y6", "z4", "x30", "x31", "z5", "h20",
    "h30", "x40", "x41", "z6", "h21", "h31", "x50", "x51", "x60", "x61", "h22", "h32", "h23", "t2", "h33",
    "t3", "o02", "o12", "o22", "o32", "o42", "o52", "o62", "o03", "o13", "o23", "o33", "o43", "o53", "o63",
)


def regroup_matrix(replicas, highs, capacity):
    rows = replicas * highs * Z * capacity
    order = np.arange(rows).reshape(replicas, highs, Z, capacity).transpose(2, 0, 1, 3).reshape(-1)
    matrix = np.zeros((rows, rows), np.float32)
    matrix[np.arange(rows), order] = 1
    return matrix


def kernel(
    sections, experts, replicas,
    cot_hbm, combine_hbm, routes_hbm, hidden_hbm, perm_hbm, out_hbm,
    cot, combine, routes, perm, slot, held, turned, *rest,
):
    n = len(CHUNKS)
    ysend, yrecv, zsend, zrecv, xsend, xrecv, own, outb = (rest[i * n:(i + 1) * n] for i in range(8))
    load_sem, ys, yr, zs, zr, xs, xr, hs, hr, out_sem = rest[8 * n:]
    highs = experts // Z
    ring = highs * replicas
    tokens, features = cot.shape
    part_rows = held.shape[3]
    share = features // replicas
    offsets = [sum(CHUNKS[:c]) for c in range(n)]

    p, e, d = lax.axis_index("pipe"), lax.axis_index("expert"), lax.axis_index("dp")
    high, z = e // Z, e % Z
    y = high * replicas + d
    mine = d * highs + high
    keep = jnp.where(p < sections // 2, 0, 1)

    def y_peer(step):
        other = (y + step) % ring
        oh, od = other // replicas, other % replicas
        return (p, oh * Z + z, od), od * highs + oh

    def z_peer(step):
        other = (z + step) % Z
        return (p, high * Z + other, d), other

    mirror = (sections - 1 - p, e, d)

    barrier = pltpu.get_barrier_semaphore()

    def greet(peer):
        pl.semaphore_signal(barrier, inc=1, device_id=peer, device_id_type=MESH)

    peers = [y_peer(s)[0] for s in RING] + [z_peer(s)[0] for s in RING] + [mirror]
    for peer in peers:
        greet(peer)

    def hidden_cols(part):
        half = part_rows * PARTS // 2
        base = (1 - keep if part < PARTS // 2 else keep) * half + part % (PARTS // 2) * part_rows
        return pl.ds(pl.multiple_of(base, part_rows), part_rows)

    loads = [
        pltpu.make_async_copy(routes_hbm, routes, load_sem.at[0]),
        pltpu.make_async_copy(combine_hbm, combine, load_sem.at[1]),
        pltpu.make_async_copy(cot_hbm, cot, load_sem.at[2]),
        pltpu.make_async_copy(perm_hbm, perm, load_sem.at[3]),
    ] + [
        pltpu.make_async_copy(hidden_hbm.at[:, hidden_cols(i)], held.at[i, d], load_sem.at[4 + i])
        for i in range(PARTS)
    ]
    for load in loads:
        load.start()

    loads[0].wait()
    chosen = routes[...]
    match = (lax.broadcasted_iota(jnp.int32, (experts, tokens), 0) == chosen).astype(jnp.float32)
    before = (
        lax.broadcasted_iota(jnp.int32, (tokens, tokens), 0)
        < lax.broadcasted_iota(jnp.int32, (tokens, tokens), 1)
    ).astype(jnp.bfloat16)
    earlier = jnp.dot(match.astype(jnp.bfloat16), before, preferred_element_type=jnp.float32)
    position = jnp.sum(earlier * match, axis=0, keepdims=True)
    slots = slot.shape[0]
    capacity = slots // experts
    target = chosen.astype(jnp.float32) * capacity + position
    slot[...] = (
        lax.broadcasted_iota(jnp.int32, (slots, tokens), 0).astype(jnp.float32) == target
    ).astype(jnp.bfloat16)
    loads[1].wait()
    eye = lax.broadcasted_iota(jnp.int32, (tokens, tokens), 0) == lax.broadcasted_iota(
        jnp.int32, (tokens, tokens), 1
    )
    weight = jnp.sum(jnp.where(eye, combine[...], 0.0), axis=1, keepdims=True)
    loads[2].wait()

    def place(c):
        w = CHUNKS[c]
        for q in range(replicas):
            at = q * share + offsets[c]
            block = (weight * cot[:, at:at + w].astype(jnp.float32)).astype(jnp.bfloat16)
            placed = jnp.dot(slot[...], block, preferred_element_type=jnp.float32).astype(jnp.bfloat16)
            for h in range(highs):
                rows = slots // highs
                ysend[c][q * highs + h] = placed[h * rows:(h + 1) * rows]

    def y_send(c):
        for step in RING:
            peer, theirs = y_peer(step)
            pltpu.make_async_remote_copy(
                src_ref=ysend[c].at[theirs], dst_ref=yrecv[c].at[mine],
                send_sem=ys.at[c], recv_sem=yr.at[c], device_id=peer, device_id_type=MESH).start()
        pltpu.make_async_copy(ysend[c].at[mine], yrecv[c].at[mine], yr.at[c]).start()

    def z_send(c):
        for step in RING:
            peer, theirs = z_peer(step)
            pltpu.make_async_remote_copy(
                src_ref=zsend[c].at[theirs], dst_ref=zrecv[c].at[z],
                send_sem=zs.at[c], recv_sem=zr.at[c], device_id=peer, device_id_type=MESH).start()
        pltpu.make_async_copy(zsend[c].at[z], zrecv[c].at[z], zr.at[c]).start()

    def wait_for(ref, sem):
        pltpu.make_async_copy(ref, ref, sem).wait()

    def flat(ref):
        return ref[...].reshape(ref.shape[0] * ref.shape[1], ref.shape[2])

    def regroup(c):
        wait_for(yrecv[c], yr.at[c])
        moved = jnp.dot(perm[...], flat(yrecv[c]), preferred_element_type=jnp.float32)
        zsend[c][...] = moved.astype(jnp.bfloat16).reshape(zsend[c].shape)

    def part_of(ref, part):
        return ref.at[pl.ds(part % (PARTS // 2) * part_rows, part_rows)]

    def x_copy(c, part):
        return pltpu.make_async_remote_copy(
            src_ref=part_of(xsend[c], part), dst_ref=part_of(xrecv[c], part),
            send_sem=xs.at[c, part], recv_sem=xr.at[c, part], device_id=mirror, device_id_type=MESH)

    def give(c, part):
        if part == 0:
            wait_for(zrecv[c], zr.at[c])
        part_of(xsend[c], part)[...] = jnp.dot(
            turned[part], flat(zrecv[c]), preferred_element_type=jnp.float32).astype(jnp.bfloat16)
        x_copy(c, part).start()

    def h_copy(part, origin, way, k):
        return pltpu.make_async_remote_copy(
            src_ref=held.at[part, origin] if k else hidden_hbm.at[:, hidden_cols(part)],
            dst_ref=held.at[part, origin],
            send_sem=hs.at[part, origin, way], recv_sem=hr.at[part, origin],
            device_id=(p, e, d + 1 if way else d - 1), device_id_type=MESH)

    def h_round(part, k):
        if k:
            @pl.when(d >= k)
            def _():
                wait_for(held.at[part, d - k], hr.at[part, d - k])

        @pl.when((d >= k) & (d < replicas - 1))
        def _():
            h_copy(part, d - k, 1, k).start()

        if k:
            @pl.when(d + k < replicas)
            def _():
                wait_for(held.at[part, d + k], hr.at[part, d + k])

        @pl.when((d + k < replicas) & (d > 0))
        def _():
            h_copy(part, d + k, 0, k).start()

    def h_sent(part, k):
        @pl.when((d >= k) & (d < replicas - 1))
        def _():
            h_copy(part, d - k, 1, k).wait_send()

        @pl.when((d + k < replicas) & (d > 0))
        def _():
            h_copy(part, d + k, 0, k).wait_send()

    def turn(part):
        loads[4 + part].wait()
        turned[part] = lax.dot_general(
            flat(held.at[part]), perm[...], (((0,), (0,)), ((), ())),
            preferred_element_type=jnp.float32).astype(jnp.bfloat16)

    def keep_own(c, part):
        part_of(own[c], part)[...] = jnp.dot(
            turned[part], flat(zrecv[c]), preferred_element_type=jnp.float32).astype(jnp.bfloat16)

    pl.semaphore_wait(barrier, len(peers))
    for step in PLAN:
        what, i = step[0], [int(digit) for digit in step[1:]]
        if what == "y":
            place(i[0])
            y_send(i[0])
        elif what == "z":
            if i[0] == 0:
                loads[3].wait()
            regroup(i[0])
            z_send(i[0])
        else:
            {"x": give, "h": h_round, "t": turn, "o": keep_own}[what](*i)

    def result(c):
        return pltpu.make_async_copy(
            outb[c], out_hbm.at[:, pl.ds(offsets[c], CHUNKS[c])], out_sem.at[c])

    for c in range(n):
        for part in range(PARTS // 2):
            wait_for(part_of(xrecv[c], part), xr.at[c, part])
        outb[c][...] = (
            own[c][...].astype(jnp.float32) + xrecv[c][...].astype(jnp.float32)
        ).astype(jnp.bfloat16)
        result(c).start()
    for c in range(n):
        wait_for(ysend[c].at[pl.ds(0, ring - 1)], ys.at[c])
        wait_for(zsend[c].at[pl.ds(0, Z - 1)], zs.at[c])
        for part in range(PARTS // 2):
            wait_for(part_of(xsend[c], part), xs.at[c, part])

    for part in range(PARTS):
        for k in range(replicas - 1):
            h_sent(part, k)
    for c in range(n):
        result(c).wait()


def solution(mesh):
    sections, experts, replicas = (mesh.shape[a] for a in ("pipe", "expert", "dp"))

    def on_device(cotangent, combine, routes, saved_hidden):
        tokens, features = cotangent.shape[1:]
        slots, hidden_units = saved_hidden.shape[3:]
        half, share = hidden_units // 2, features // replicas
        highs = experts // Z
        rows = slots * replicas
        capacity = slots // experts
        matrix = regroup_matrix(replicas, highs, capacity)
        perm = jnp.asarray(matrix, jnp.bfloat16)
        n = len(CHUNKS)
        bf16 = jnp.bfloat16
        dma = pltpu.SemaphoreType.DMA
        each = lambda lead: [pltpu.VMEM(lead + (w,), bf16) for w in CHUNKS]
        block = (replicas * highs, rows // (replicas * highs))
        zblock = (Z, rows // Z)
        out = pl.pallas_call(
            functools.partial(kernel, sections, experts, replicas),
            out_shape=jax.ShapeDtypeStruct((half, share), bf16),
            in_specs=[pl.BlockSpec(memory_space=pl.ANY)] * 5,
            out_specs=pl.BlockSpec(memory_space=pl.ANY),
            scratch_shapes=[
                pltpu.VMEM((tokens, features), bf16),
                pltpu.VMEM((1, tokens), jnp.float32),
                pltpu.VMEM((1, tokens), jnp.int32),
                pltpu.VMEM((rows, rows), bf16),
                pltpu.VMEM((slots, tokens), bf16),
                pltpu.VMEM((PARTS, replicas, slots, hidden_units // PARTS), bf16),
                pltpu.VMEM((PARTS, hidden_units // PARTS, rows), bf16),
                *each(block), *each(block), *each(zblock), *each(zblock),
                *each((half,)), *each((half,)), *each((half,)), *each((half,)),
                dma((4 + PARTS,)),
                dma((n,)), dma((n,)), dma((n,)), dma((n,)),
                dma((n, PARTS // 2)), dma((n, PARTS // 2)),
                dma((PARTS, replicas, 2)), dma((PARTS, replicas)),
                dma((n,)),
            ],
            compiler_params=pltpu.CompilerParams(
                collective_id=0, has_side_effects=True, vmem_limit_bytes=60 << 20),
        )(
            cotangent[0], combine.reshape(1, tokens), routes.reshape(1, tokens),
            saved_hidden[0, 0, 0], perm,
        )
        return out[None, None]

    return jax.shard_map(
        on_device,
        mesh=mesh,
        in_specs=(
            P("pipe", ("expert", "dp"), None),
            P("pipe", ("expert", "dp"), None),
            P("pipe", ("expert", "dp"), None),
            P("pipe", "expert", "dp", None, None),
        ),
        out_specs=P("pipe", "expert", None, "dp"),
        check_vma=False,
    )
```

```python
import functools

import jax
import jax.numpy as jnp
import numpy as np
from jax import lax
from jax.experimental import pallas as pl
from jax.experimental.pallas import tpu as pltpu
from jax.sharding import PartitionSpec as P

MESH = pl.DeviceIdType.MESH
CHUNKS = (128,) * 7
PARTS = 4
RING = (1, 7, 2, 6, 3, 5, 4)
Z = 8
PLAN = (
    "h00", "h10", "y0", "y1", "h01", "h11", "y2", "h02", "h12", "z0", "y3", "z1", "h03", "t0", "h13", "t1",
    "x00", "x01", "y4", "z2", "x10", "x11", "y5", "z3", "x20", "x21", "y6", "z4", "x30", "x31", "z5", "h20",
    "h30", "x40", "x41", "z6", "h21", "h31", "x50", "x51", "x60", "x61", "h22", "h32", "h23", "t2", "h33",
    "t3", "o0", "o1", "o2", "o3", "o4", "o5", "o6",
)


def regroup_matrix(replicas, highs, capacity):
    rows = replicas * highs * Z * capacity
    order = np.arange(rows).reshape(replicas, highs, Z, capacity).transpose(2, 0, 1, 3).reshape(-1)
    matrix = np.zeros((rows, rows), np.float32)
    matrix[np.arange(rows), order] = 1
    return matrix


def kernel(
    sections, experts, replicas,
    cot_hbm, combine_hbm, routes_hbm, hidden_hbm, perm_hbm, out_hbm,
    cot, combine, routes, perm, slot, held, turned, *rest,
):
    n = len(CHUNKS)
    ysend, yrecv, zsend, zrecv, xsend, xrecv, own, outb = (rest[i * n:(i + 1) * n] for i in range(8))
    load_sem, ys, yr, zs, zr, xs, xr, hs, hr, out_sem = rest[8 * n:]
    highs = experts // Z
    ring = highs * replicas
    tokens, features = cot.shape
    part_rows = held.shape[3]
    share = features // replicas
    offsets = [sum(CHUNKS[:c]) for c in range(n)]

    p, e, d = lax.axis_index("pipe"), lax.axis_index("expert"), lax.axis_index("dp")
    high, z = e // Z, e % Z
    y = high * replicas + d
    mine = d * highs + high
    keep = jnp.where(p < sections // 2, 0, 1)

    def y_peer(step):
        other = (y + step) % ring
        oh, od = other // replicas, other % replicas
        return (p, oh * Z + z, od), od * highs + oh

    def z_peer(step):
        other = (z + step) % Z
        return (p, high * Z + other, d), other

    mirror = (sections - 1 - p, e, d)

    barrier = pltpu.get_barrier_semaphore()

    def greet(peer):
        pl.semaphore_signal(barrier, inc=1, device_id=peer, device_id_type=MESH)

    peers = [y_peer(s)[0] for s in RING] + [z_peer(s)[0] for s in RING] + [mirror]
    for peer in peers:
        greet(peer)

    def hidden_cols(part):
        half = part_rows * PARTS // 2
        base = (1 - keep if part < PARTS // 2 else keep) * half + part % (PARTS // 2) * part_rows
        return pl.ds(pl.multiple_of(base, part_rows), part_rows)

    loads = [
        pltpu.make_async_copy(routes_hbm, routes, load_sem.at[0]),
        pltpu.make_async_copy(combine_hbm, combine, load_sem.at[1]),
        pltpu.make_async_copy(cot_hbm, cot, load_sem.at[2]),
        pltpu.make_async_copy(perm_hbm, perm, load_sem.at[3]),
    ] + [
        pltpu.make_async_copy(hidden_hbm.at[:, hidden_cols(i)], held.at[i, d], load_sem.at[4 + i])
        for i in range(PARTS)
    ]
    for load in loads:
        load.start()

    loads[0].wait()
    chosen = routes[...]
    match = (lax.broadcasted_iota(jnp.int32, (experts, tokens), 0) == chosen).astype(jnp.float32)
    before = (
        lax.broadcasted_iota(jnp.int32, (tokens, tokens), 0)
        < lax.broadcasted_iota(jnp.int32, (tokens, tokens), 1)
    ).astype(jnp.bfloat16)
    earlier = jnp.dot(match.astype(jnp.bfloat16), before, preferred_element_type=jnp.float32)
    position = jnp.sum(earlier * match, axis=0, keepdims=True)
    slots = slot.shape[0]
    capacity = slots // experts
    target = chosen.astype(jnp.float32) * capacity + position
    slot[...] = (
        lax.broadcasted_iota(jnp.int32, (slots, tokens), 0).astype(jnp.float32) == target
    ).astype(jnp.bfloat16)
    loads[1].wait()
    eye = lax.broadcasted_iota(jnp.int32, (tokens, tokens), 0) == lax.broadcasted_iota(
        jnp.int32, (tokens, tokens), 1
    )
    weight = jnp.sum(jnp.where(eye, combine[...], 0.0), axis=1, keepdims=True)
    loads[2].wait()

    def place(c):
        w = CHUNKS[c]
        for q in range(replicas):
            at = q * share + offsets[c]
            block = (weight * cot[:, at:at + w].astype(jnp.float32)).astype(jnp.bfloat16)
            placed = jnp.dot(slot[...], block, preferred_element_type=jnp.float32).astype(jnp.bfloat16)
            for h in range(highs):
                rows = slots // highs
                ysend[c][q * highs + h] = placed[h * rows:(h + 1) * rows]

    def y_send(c):
        for step in RING:
            peer, theirs = y_peer(step)
            pltpu.make_async_remote_copy(
                src_ref=ysend[c].at[theirs], dst_ref=yrecv[c].at[mine],
                send_sem=ys.at[c], recv_sem=yr.at[c], device_id=peer, device_id_type=MESH).start()
        pltpu.make_async_copy(ysend[c].at[mine], yrecv[c].at[mine], yr.at[c]).start()

    def z_send(c):
        for step in RING:
            peer, theirs = z_peer(step)
            pltpu.make_async_remote_copy(
                src_ref=zsend[c].at[theirs], dst_ref=zrecv[c].at[z],
                send_sem=zs.at[c], recv_sem=zr.at[c], device_id=peer, device_id_type=MESH).start()
        pltpu.make_async_copy(zsend[c].at[z], zrecv[c].at[z], zr.at[c]).start()

    def wait_for(ref, sem):
        pltpu.make_async_copy(ref, ref, sem).wait()

    def flat(ref):
        return ref[...].reshape(ref.shape[0] * ref.shape[1], ref.shape[2])

    def regroup(c):
        wait_for(yrecv[c], yr.at[c])
        moved = jnp.dot(perm[...], flat(yrecv[c]), preferred_element_type=jnp.float32)
        zsend[c][...] = moved.astype(jnp.bfloat16).reshape(zsend[c].shape)

    def part_of(ref, part):
        return ref.at[pl.ds(part % (PARTS // 2) * part_rows, part_rows)]

    def x_copy(c, part):
        return pltpu.make_async_remote_copy(
            src_ref=part_of(xsend[c], part), dst_ref=part_of(xrecv[c], part),
            send_sem=xs.at[c, part], recv_sem=xr.at[c, part], device_id=mirror, device_id_type=MESH)

    def give(c, part):
        if part == 0:
            wait_for(zrecv[c], zr.at[c])
        part_of(xsend[c], part)[...] = jnp.dot(
            turned[part], flat(zrecv[c]), preferred_element_type=jnp.float32).astype(jnp.bfloat16)
        x_copy(c, part).start()

    def h_copy(part, origin, way, k):
        return pltpu.make_async_remote_copy(
            src_ref=held.at[part, origin] if k else hidden_hbm.at[:, hidden_cols(part)],
            dst_ref=held.at[part, origin],
            send_sem=hs.at[part, origin, way], recv_sem=hr.at[part, origin],
            device_id=(p, e, d + 1 if way else d - 1), device_id_type=MESH)

    def h_round(part, k):
        if k:
            @pl.when(d >= k)
            def _():
                wait_for(held.at[part, d - k], hr.at[part, d - k])

        @pl.when((d >= k) & (d < replicas - 1))
        def _():
            h_copy(part, d - k, 1, k).start()

        if k:
            @pl.when(d + k < replicas)
            def _():
                wait_for(held.at[part, d + k], hr.at[part, d + k])

        @pl.when((d + k < replicas) & (d > 0))
        def _():
            h_copy(part, d + k, 0, k).start()

    def h_sent(part, k):
        @pl.when((d >= k) & (d < replicas - 1))
        def _():
            h_copy(part, d - k, 1, k).wait_send()

        @pl.when((d + k < replicas) & (d > 0))
        def _():
            h_copy(part, d + k, 0, k).wait_send()

    def turn(part):
        loads[4 + part].wait()
        turned[part] = lax.dot_general(
            flat(held.at[part]), perm[...], (((0,), (0,)), ((), ())),
            preferred_element_type=jnp.float32).astype(jnp.bfloat16)

    def keep_own(c):
        rows = (PARTS - PARTS // 2) * part_rows
        table = turned[PARTS // 2:PARTS].reshape(rows, turned.shape[2])
        own[c][...] = jnp.dot(table, flat(zrecv[c]), preferred_element_type=jnp.float32).astype(jnp.bfloat16)

    pl.semaphore_wait(barrier, len(peers))
    for step in PLAN:
        what, i = step[0], [int(digit) for digit in step[1:]]
        if what == "y":
            place(i[0])
            y_send(i[0])
        elif what == "z":
            if i[0] == 0:
                loads[3].wait()
            regroup(i[0])
            z_send(i[0])
        else:
            {"x": give, "h": h_round, "t": turn, "o": keep_own}[what](*i)

    def result(c):
        return pltpu.make_async_copy(
            outb[c], out_hbm.at[:, pl.ds(offsets[c], CHUNKS[c])], out_sem.at[c])

    for c in range(n):
        for part in range(PARTS // 2):
            wait_for(part_of(xrecv[c], part), xr.at[c, part])
        outb[c][...] = (
            own[c][...].astype(jnp.float32) + xrecv[c][...].astype(jnp.float32)
        ).astype(jnp.bfloat16)
        result(c).start()
    for c in range(n):
        wait_for(ysend[c].at[pl.ds(0, ring - 1)], ys.at[c])
        wait_for(zsend[c].at[pl.ds(0, Z - 1)], zs.at[c])
        for part in range(PARTS // 2):
            wait_for(part_of(xsend[c], part), xs.at[c, part])

    for part in range(PARTS):
        for k in range(replicas - 1):
            h_sent(part, k)
    for c in range(n):
        result(c).wait()


def solution(mesh):
    sections, experts, replicas = (mesh.shape[a] for a in ("pipe", "expert", "dp"))

    def on_device(cotangent, combine, routes, saved_hidden):
        tokens, features = cotangent.shape[1:]
        slots, hidden_units = saved_hidden.shape[3:]
        half, share = hidden_units // 2, features // replicas
        highs = experts // Z
        rows = slots * replicas
        capacity = slots // experts
        matrix = regroup_matrix(replicas, highs, capacity)
        perm = jnp.asarray(matrix, jnp.bfloat16)
        n = len(CHUNKS)
        bf16 = jnp.bfloat16
        dma = pltpu.SemaphoreType.DMA
        each = lambda lead: [pltpu.VMEM(lead + (w,), bf16) for w in CHUNKS]
        block = (replicas * highs, rows // (replicas * highs))
        zblock = (Z, rows // Z)
        out = pl.pallas_call(
            functools.partial(kernel, sections, experts, replicas),
            out_shape=jax.ShapeDtypeStruct((half, share), bf16),
            in_specs=[pl.BlockSpec(memory_space=pl.ANY)] * 5,
            out_specs=pl.BlockSpec(memory_space=pl.ANY),
            scratch_shapes=[
                pltpu.VMEM((tokens, features), bf16),
                pltpu.VMEM((1, tokens), jnp.float32),
                pltpu.VMEM((1, tokens), jnp.int32),
                pltpu.VMEM((rows, rows), bf16),
                pltpu.VMEM((slots, tokens), bf16),
                pltpu.VMEM((PARTS, replicas, slots, hidden_units // PARTS), bf16),
                pltpu.VMEM((PARTS, hidden_units // PARTS, rows), bf16),
                *each(block), *each(block), *each(zblock), *each(zblock),
                *each((half,)), *each((half,)), *each((half,)), *each((half,)),
                dma((4 + PARTS,)),
                dma((n,)), dma((n,)), dma((n,)), dma((n,)),
                dma((n, PARTS // 2)), dma((n, PARTS // 2)),
                dma((PARTS, replicas, 2)), dma((PARTS, replicas)),
                dma((n,)),
            ],
            compiler_params=pltpu.CompilerParams(
                collective_id=0, has_side_effects=True, vmem_limit_bytes=60 << 20),
        )(
            cotangent[0], combine.reshape(1, tokens), routes.reshape(1, tokens),
            saved_hidden[0, 0, 0], perm,
        )
        return out[None, None]

    return jax.shard_map(
        on_device,
        mesh=mesh,
        in_specs=(
            P("pipe", ("expert", "dp"), None),
            P("pipe", ("expert", "dp"), None),
            P("pipe", ("expert", "dp"), None),
            P("pipe", "expert", "dp", None, None),
        ),
        out_specs=P("pipe", "expert", None, "dp"),
        check_vma=False,
    )
```
